128 devices in a mesh: tp: 8 (over x_hi, y), fsdp: 16 (over z, x_lo, core).
Axes of the slice: x: 4 (x_hi: 2, x_lo: 2; x = x_hi * 2 + x_lo), y: 4, z: 4, core: 2. Of those that a mesh axis runs over, the one named last changes fastest.
Arguments:
- attn_out: bfloat16 [2048, 16384], P('fsdp', 'tp')
- w_out: bfloat16 [16384, 16384], P('tp', 'fsdp')
- student: bfloat16 [2048, 8192], P('fsdp', 'tp')
- w_align: bfloat16 [8192, 16384], P('tp', 'fsdp')
- perm: int32 [2048], replicated, may hold values from 0 to 2047, as said below
Outputs:
- loss: float32 [], replicated
- grad_align: float32 [8192, 16384], P('tp', 'fsdp')
The draws below stay inside these ranges and needn't reach their ends.
Inputs may be any that keep to these rules, and one draw needn't show every extreme that they name: `perm`: each of the 2048 teacher tokens is named by exactly one student row.
All inputs are finite; a program needn't handle non-finite values.
Results may differ from the reference program's by a relative error of at most 0.0049.
Values may be sent and summed in bfloat16 or wider, within the bound.
A program may use at most 128 MiB of HBM per device.

```python
import math
import jax
import jax.numpy as jnp
from jax import lax

H = 16384
S = 8192
TOKENS = 2048


def shared_rows(key, spread):
    base = jnp.clip(jax.random.normal(jax.random.fold_in(key, 101), (TOKENS, S), jnp.float32), -6.0, 6.0)
    row_scale = jnp.exp(spread * jax.random.uniform(jax.random.fold_in(key, 102), (TOKENS, 1), jnp.float32))
    return (base, row_scale)


def alignment(key):
    return jax.random.permutation(jax.random.fold_in(key, 103), TOKENS).astype(jnp.int32)


def head_rows(key):
    return jnp.clip(jax.random.normal(jax.random.fold_in(key, 104), (S, H), jnp.float32), -6.0, 6.0) / math.sqrt(H)


def draw_attn_out(key, part):
    spread = 0.0
    far_scale = 0.5
    shared, row_scale = shared_rows(key, spread)
    key = jax.random.fold_in(key, 1)
    rest = far_scale * jnp.clip(jax.random.normal(key, (TOKENS, H - S), jnp.float32), -6.0, 6.0)
    return jnp.concatenate([shared, rest], axis=1).astype(jnp.bfloat16)


def draw_student(key, part):
    spread = 0.0
    low_noise = 0.1
    high_noise = 5.0
    shared, row_scale = shared_rows(key, spread)
    order = alignment(key)
    key = jax.random.fold_in(key, 2)
    position = jnp.arange(TOKENS, dtype=jnp.float32)[:, None] / TOKENS
    rough = jnp.exp(jax.random.uniform(jax.random.fold_in(key, 5), (TOKENS, 1), jnp.float32, math.log(0.7), math.log(1.4)))
    noise_scale = low_noise * jnp.exp(position * math.log(high_noise / low_noise)) * rough
    noise = jnp.clip(jax.random.normal(key, (TOKENS, S), jnp.float32), -6.0, 6.0)
    picked = jnp.take(shared, order, axis=0)
    picked_scale = jnp.take(row_scale, order, axis=0)
    return (picked + noise_scale * noise * picked_scale).astype(jnp.bfloat16)


def draw_w_out(key, part):
    upper = head_rows(key)
    key = jax.random.fold_in(key, 3)
    lower = jnp.clip(jax.random.normal(key, (H - S, H), jnp.float32), -6.0, 6.0) / math.sqrt(H)
    return jnp.concatenate([upper, lower], axis=0).astype(jnp.bfloat16)


def draw_w_align(key, part):
    upper = head_rows(key)
    key = jax.random.fold_in(key, 4)
    noise = jnp.clip(jax.random.normal(key, (S, H), jnp.float32), -6.0, 6.0) / math.sqrt(S)
    return (2.0 * upper + 0.25 * noise).astype(jnp.bfloat16)


def draw_perm(key, part):
    order = alignment(key)
    return order


def setup_inputs(seed: int = 0) -> dict:
    arg_keys = jax.random.split(jax.random.key(seed), 6)
    attn_out = draw_attn_out(jax.random.fold_in(arg_keys[5], 71), 0)
    w_out = draw_w_out(jax.random.fold_in(arg_keys[5], 71), 0)
    student = draw_student(jax.random.fold_in(arg_keys[5], 71), 0)
    w_align = draw_w_align(jax.random.fold_in(arg_keys[5], 71), 0)
    perm = draw_perm(jax.random.fold_in(arg_keys[5], 71), 0)
    return dict(attn_out=attn_out, w_out=w_out, student=student, w_align=w_align, perm=perm)


def reference(attn_out, w_out, student, w_align, perm):
    teacher = jnp.dot(attn_out, w_out, preferred_element_type=jnp.float32).astype(jnp.bfloat16)
    target = jnp.take(teacher, perm, axis=0)
    pred = jnp.dot(student, w_align, preferred_element_type=jnp.float32)
    target32 = target.astype(jnp.float32)
    dots = lax.optimization_barrier(jnp.sum(pred * target32, axis=1))
    sq_pred = lax.optimization_barrier(jnp.sum(pred * pred, axis=1))
    sq_target = lax.optimization_barrier(jnp.sum(target32 * target32, axis=1))
    norm_pred = jnp.sqrt(sq_pred + 1e-06)
    norm_target = jnp.sqrt(sq_target + 1e-06)
    cosine = dots / (norm_pred * norm_target)
    loss = jnp.sum(1.0 - cosine) / TOKENS
    scale = H / 32.0
    grad_pred = (-scale * (target32 / (norm_pred * norm_target)[:, None] - (cosine / (norm_pred * norm_pred))[:, None] * pred)).astype(jnp.bfloat16)
    grad_align = jnp.dot(student.T, grad_pred, preferred_element_type=jnp.float32)
    return (loss, grad_align)
```

```python
import functools

import jax
import jax.numpy as jnp
from jax import lax
from jax.experimental import pallas as pl
from jax.experimental.pallas import tpu as pltpu
from jax.sharding import PartitionSpec as P

MESH = pl.DeviceIdType.MESH
BF, F32 = jnp.bfloat16, jnp.float32

NC = 8
CH = 256
BL = 128
GR = 64
HF = 32
D1, D2, D3, D4, D5, D6, D7 = 1, 2, 3, 4, 5, 6, 7
LAST = 2 * NC - 1


def place():
    t, f = lax.axis_index("tp"), lax.axis_index("fsdp")
    return t // 4, t % 4, f // 4, (f // 2) % 2, f % 2, t, f


def kernel(attn_in, stu_in, wout_in, wal_in, perm_ref, loss_ref, grad_out,
           attn, stu, stup, wout, wal, part, rsend, rrecv, nsend, nrecv, xsend, xrecv, keep,
           town, pown, ssend, srecv, gall, acc, lacc, lrecv,
           sem_in, sem_as, sem_ar, sem_ss, sem_sr, sem_rs, sem_rr, sem_ns, sem_nr, sem_xs, sem_xr,
           sem_ts, sem_tr, sem_gs, sem_gr, sem_fs, sem_fr, sem_ls, sem_lr):
    xh, y, z, xl, c, t, f = place()
    total_rows = NC * CH

    def tp_dev(a, b):
        return {"tp": a * 4 + b, "fsdp": f}

    def fs_dev(a, b, d):
        return {"tp": t, "fsdp": a * 4 + b * 2 + d}

    zp, zm, z2 = (z + 1) % 4, (z + 3) % 4, (z + 2) % 4
    yp, ym = (y + 1) % 4, (y + 3) % 4
    y2 = (y + 2) % 4
    xo, ho, co = 1 - xl, 1 - xh, 1 - c
    Y_UP, Y_DN, X_HI = tp_dev(xh, yp), tp_dev(xh, ym), tp_dev(ho, y)
    Z_UP, Z_DN = fs_dev(zp, xl, c), fs_dev(zm, xl, c)
    X_LO, CORE = fs_dev(z, xo, c), fs_dev(z, xl, co)

    def remote(src, dst, ss, rs, dev):
        return pltpu.make_async_remote_copy(
            src_ref=src, dst_ref=dst, send_sem=ss, recv_sem=rs, device_id=dev, device_id_type=MESH)

    def rows(a, b, d):
        return (a * 4 + b * 2 + d) * BL

    own = rows(z, xl, c)
    loads = [
        pltpu.make_async_copy(attn_in, attn.at[pl.ds(own, BL)], sem_in.at[0]),
        pltpu.make_async_copy(wout_in, wout, sem_in.at[1]),
        pltpu.make_async_copy(stu_in, stu.at[pl.ds(own, BL)], sem_in.at[2]),
        pltpu.make_async_copy(wal_in, wal, sem_in.at[3]),
    ]
    for l in loads:
        l.start()

    barrier = pltpu.get_barrier_semaphore()
    for i in range(1, 16):
        pl.semaphore_signal(barrier, inc=1, device_id={"tp": t, "fsdp": (f + i) % 16}, device_id_type=MESH)
    for i in range(1, 8):
        pl.semaphore_signal(barrier, inc=1, device_id={"tp": (t + i) % 8, "fsdp": f}, device_id_type=MESH)
    pl.semaphore_wait(barrier, 22)

    blk = [(z, xl), (z, xo), (zm, xl), (zp, xl), (zm, xo), (zp, xo), (z2, xl), (z2, xo)]

    def a_rows(k, d=None, off=0, n=BL):
        return attn.at[pl.ds(rows(blk[k][0], blk[k][1], c if d is None else d) + off, n)]

    def s_rows(k, d=None, off=0, n=BL):
        return stu.at[pl.ds(rows(blk[k][0], blk[k][1], c if d is None else d) + off, n)]

    HB = BL // 2

    def a_own(src_ref, j, dev, peer_slot):
        return remote(attn_in, a_rows(0), sem_as.at[j], sem_ar.at[peer_slot], dev)

    def a_recv(k):
        return remote(a_rows(k), a_rows(k), sem_as.at[0], sem_ar.at[k], X_LO)

    def half_recv(ref_rows, k, h, sems, slot):
        r = ref_rows(k, None, h * HB, HB)
        return remote(r, r, sem_as.at[0], sems.at[slot], X_LO)

    def core_copies(ref_rows, k, send, ssem, rsem, slot):
        n = BL // 4
        out = []
        for i in range(4):
            r = ref_rows(k, None, i * n, n)
            out.append(remote(r, r, ssem.at[slot], rsem.at[slot], CORE))
        return out

    def core_whole(ref_rows, k, ssem, rsem, slot):
        r = ref_rows(k, co)
        return remote(r, r, ssem.at[slot], rsem.at[slot], CORE)

    sends = {}

    def go(name, copy):
        copy().start()
        sends[name] = copy

    s_src = stu_in
    go("a0", lambda: remote(attn_in, a_rows(0), sem_as.at[0], sem_ar.at[1], X_LO))
    go("a1", lambda: remote(attn_in, a_rows(0), sem_as.at[1], sem_ar.at[2], Z_UP))
    go("a2", lambda: remote(attn_in, a_rows(0), sem_as.at[2], sem_ar.at[3], Z_DN))
    loads[0].wait()

    def to_core(ref_rows, k, ssem, rsem, slot):
        for cp in core_copies(ref_rows, k, None, ssem, rsem, slot):
            cp.start()
        sends[ref_rows, k] = lambda: remote(ref_rows(k), ref_rows(k), ssem.at[slot], rsem.at[slot], CORE)

    to_core(a_rows, 0, sem_as, sem_ar, 10)
    go("s0", lambda: remote(stu_in, s_rows(0), sem_ss.at[0], sem_sr.at[0], Z_UP))
    go("s1", lambda: remote(stu_in, s_rows(0), sem_ss.at[1], sem_sr.at[1], Z_DN))
    go("s2", lambda: remote(stu_in, s_rows(0), sem_ss.at[2], sem_sr.at[4], X_LO))
    loads[2].wait()
    to_core(s_rows, 0, sem_ss, sem_sr, 8)
    loads[1].wait()
    loads[3].wait()
    acc[...] = jnp.zeros_like(acc)
    lacc[...] = jnp.zeros_like(lacc)

    def arrive_a(k):
        if k < 6:
            a_recv(k).wait_recv()
        else:
            half_recv(a_rows, k, 0, sem_ar, 6 + 2 * (k - 6)).wait_recv()
            half_recv(a_rows, k, 1, sem_ar, 7 + 2 * (k - 6)).wait_recv()
        if k == 1:
            go("a3", lambda: remote(a_rows(1), a_rows(1), sem_as.at[3], sem_ar.at[4], Z_UP))
            go("a4", lambda: remote(a_rows(1), a_rows(1), sem_as.at[4], sem_ar.at[5], Z_DN))
        if k in (2, 4):
            go(f"u{k}", lambda: remote(a_rows(k, None, 0, HB), a_rows(k, None, 0, HB),
                                       sem_as.at[5 + (k - 2) // 2], sem_ar.at[6 + (k - 2)], Z_UP))
        if k in (3, 5):
            go(f"d{k}", lambda: remote(a_rows(k, None, HB, HB), a_rows(k, None, HB, HB),
                                       sem_as.at[7 + (k - 3) // 2], sem_ar.at[7 + (k - 3)], Z_DN))
        to_core(a_rows, k, sem_as, sem_ar, 10 + k)

    def arrive_s(step):
        if step == 0:
            for k, slot, dev, off, out in ((2, 0, Z_UP, 0, 2), (3, 1, Z_DN, HB, 3)):
                remote(s_rows(k), s_rows(k), sem_ss.at[0], sem_sr.at[slot], X_LO).wait_recv()
                go(f"h{k}", lambda k=k, off=off, out=out, dev=dev: remote(
                    s_rows(k, None, off, HB), s_rows(k, None, off, HB), sem_ss.at[1 + out], sem_sr.at[out], dev))
                go(f"x{k}", lambda k=k, out=out: remote(
                    s_rows(k), s_rows(k), sem_ss.at[3 + out], sem_sr.at[3 + out], X_LO))
                to_core(s_rows, k, sem_ss, sem_sr, 8 + k)
        elif step == 1:
            half_recv(s_rows, 6, 0, sem_sr, 2).wait_recv()
            half_recv(s_rows, 6, 1, sem_sr, 3).wait_recv()
            go("x6", lambda: remote(s_rows(6), s_rows(6), sem_ss.at[7], sem_sr.at[7], X_LO))
            to_core(s_rows, 6, sem_ss, sem_sr, 8 + 6)
        else:
            for k, slot in ((1, 4), (4, 5), (5, 6), (7, 7)):
                remote(s_rows(k), s_rows(k), sem_ss.at[0], sem_sr.at[slot], X_LO).wait_recv()
                to_core(s_rows, k, sem_ss, sem_sr, 8 + k)

    def core_arrived(ref_rows, k, ssem, rsem, slot):
        core_whole(ref_rows, k, ssem, rsem, slot).wait_recv()

    def group(ref, slot, g, off, n):
        return ref[slot, pl.ds(g * GR + off, n), :]

    def relay(r, d):
        s = r % 4
        dev = Y_UP if d == 0 else Y_DN
        return remote(rsend.at[s, d], rrecv.at[r, d], sem_rs.at[s, d], sem_rr.at[r, d], dev)

    def near(r, d):
        s = r % 4
        dev = Y_UP if d == 0 else Y_DN
        return remote(nsend.at[s, d], nrecv.at[r, d], sem_ns.at[s, d], sem_nr.at[r, d], dev)

    def across(r):
        s = r % 4
        return remote(xsend.at[s], xrecv.at[r], sem_xs.at[s], sem_xr.at[r], X_HI)

    def stage0_send(r):
        s = r % 4
        rsend[s, 0] = group(part, s, y2, 0, HF).astype(BF)
        relay(r, 0).start()
        rsend[s, 1] = group(part, s, y2, HF, HF).astype(BF)
        relay(r, 1).start()

    def stage0_teacher(r, k):
        core_arrived(a_rows, k, sem_as, sem_ar, 10 + k)
        base = (blk[k][0] * 2 + blk[k][1]) * CH
        part[r % 4] = jnp.dot(attn[pl.ds(base, CH), :], wout[...], preferred_element_type=F32)

    def stage0_student(r):
        base = pl.multiple_of((r - NC) * CH, CH)
        row = lax.broadcasted_iota(jnp.int32, (CH, total_rows), 0) + base
        pick = jnp.where(row == perm_ref[...], 1.0, 0.0).astype(BF)
        mine = jnp.dot(pick, stu[...], preferred_element_type=F32).astype(BF)
        stup[pl.ds(base, CH), :] = mine
        part[r % 4] = jnp.dot(mine, wal[...], preferred_element_type=F32)

    def stage1(r):
        s = r % 4
        relay(r, 0).wait()
        nsend[s, 0, 0:HF, :] = (group(part, s, yp, 0, HF) + rrecv[r, 0].astype(F32)).astype(BF)
        nsend[s, 0, HF:GR, :] = group(part, s, yp, HF, HF).astype(BF)
        near(r, 0).start()
        relay(r, 1).wait()
        nsend[s, 1, 0:HF, :] = group(part, s, ym, 0, HF).astype(BF)
        nsend[s, 1, HF:GR, :] = (group(part, s, ym, HF, HF) + rrecv[r, 1].astype(F32)).astype(BF)
        near(r, 1).start()

    def stage2(r):
        s = r % 4
        near(r, 0).wait()
        near(r, 1).wait()

        def half(h):
            o = pl.multiple_of(h * HF, HF)
            return (group(part, s, y, o, HF) + nrecv[r, 0, pl.ds(o, HF), :].astype(F32)
                    + nrecv[r, 1, pl.ds(o, HF), :].astype(F32))

        xsend[s] = half(ho)
        across(r).start()
        keep[s] = half(xh)

    def stat_copy(k, i):
        return remote(ssend.at[k], srecv.at[k, f], sem_ts.at[k], sem_tr.at[k],
                      {"tp": t, "fsdp": (f + i) % 16})

    def lanes_of(cols):
        lane = lax.broadcasted_iota(jnp.int32, (HF, 128), 1)
        m = jnp.zeros((HF, 128), F32)
        for j, col in enumerate(cols):
            m = jnp.where(lane == j, col, m)
        m = jnp.concatenate([m, jnp.zeros((128 - HF, 128), F32)], axis=0)
        return m.T[0:8, :]

    def stage3(r):
        s = r % 4
        across(r).wait()
        full = keep[s] + xrecv[r]

        @pl.when(r < NC)
        def _():
            j = r // 2
            dz = jnp.where(r < 2, 0, jnp.where(r >= 6, 2, jnp.where(r % 2 == 0, 3, 1)))
            other = jnp.where(r < 2, r, jnp.where(r >= 6, r - 6, (r - 2) // 2))
            q = ((z + dz) % 4) * 2 + jnp.where(other == 0, xl, xo)
            town[q] = full.astype(BF)

        @pl.when(r >= NC)
        def _():
            k = r - NC
            tg = town[k].astype(F32)
            pown[k] = full
            ssend[k] = lanes_of([jnp.sum(full * tg, axis=1, keepdims=True),
                                 jnp.sum(full * full, axis=1, keepdims=True),
                                 jnp.sum(tg * tg, axis=1, keepdims=True)])
            srecv[k, f] = ssend[k]
            for i in range(1, 16):
                stat_copy(k, i).start()

    def g_rows(k, g, h):
        return gall.at[pl.ds(pl.multiple_of(k * CH + g * GR + h * HF, HF), HF)]

    def g_across(k, h):
        return remote(g_rows(k, y, h), g_rows(k, y, h), sem_xs.at[4 + k % 4], sem_xr.at[2 * NC + k], X_HI)

    def g_near(k, d, h, g):
        return remote(g_rows(k, g, h), g_rows(k, g, h), sem_gs.at[k % 4, d, h], sem_gr.at[k, d, h],
                      Y_UP if d == 0 else Y_DN)

    def g_far(k, d, g):
        return remote(g_rows(k, g, d), g_rows(k, g, d), sem_fs.at[k % 4, d], sem_fr.at[k, d],
                      Y_UP if d == 0 else Y_DN)

    def stage4(k):
        w = remote(srecv.at[k, pl.ds(0, 15)], srecv.at[k, pl.ds(0, 15)], sem_ts.at[k], sem_tr.at[k], CORE)
        w.wait_recv()
        w.wait_send()
        st = srecv[k, 0]
        for i in range(1, 16):
            st = st + srecv[k, i]
        dots, pp, qq = st[0:1, :], st[1:2, :], st[2:3, :]
        n_p, n_t = jnp.sqrt(pp + 1e-6), jnp.sqrt(qq + 1e-6)
        cosine = dots / (n_p * n_t)
        lane = lax.broadcasted_iota(jnp.int32, (1, 128), 1)
        lacc[0:1, :] += jnp.where(lane < HF, 1.0 - cosine, 0.0)
        scale = 16 * 1024 / 32.0
        ca = -scale / (n_p * n_t)
        cb = scale * (cosine / (n_p * n_p))
        both = jnp.concatenate([ca, cb, jnp.zeros((126, 128), F32)], axis=0).T
        g = both[0:HF, 0:1] * town[k].astype(F32) + both[0:HF, 1:2] * pown[k]
        gall[pl.ds(pl.multiple_of(k * CH + y * GR + xh * HF, HF), HF), :] = g.astype(BF)
        g_across(k, xh).start()
        g_near(k, 0, xh, y).start()
        g_near(k, 1, xh, y).start()

    def stage5(k):
        g_across(k, xh).wait_send()
        g_across(k, ho).wait_recv()
        g_near(k, 0, ho, y).start()
        g_near(k, 1, ho, y).start()

    def stage6(k):
        g_near(k, 0, 0, ym).wait_recv()
        g_far(k, 0, ym).start()
        g_near(k, 1, 1, yp).wait_recv()
        g_far(k, 1, yp).start()

    def stage7(k):
        g_near(k, 0, 1, ym).wait_recv()
        g_near(k, 1, 0, yp).wait_recv()
        g_far(k, 0, y2).wait_recv()
        g_far(k, 1, y2).wait_recv()
        for d in range(2):
            g_far(k, d, y).wait_send()
            for h in range(2):
                g_near(k, d, h, y).wait_send()
        base = pl.multiple_of(k * CH, CH)
        acc[...] += lax.dot_general(
            stup[pl.ds(base, CH), :], gall[pl.ds(base, CH), :], (((0,), (0,)), ((), ())),
            preferred_element_type=F32)

    def tick(i, carry):
        def when(lo, hi, cond_value):
            return pl.when(jnp.logical_and(cond_value >= lo, cond_value <= hi))

        for d, fn in ((D6, stage6), (D5, stage5), (D4, stage4)):
            @when(NC, LAST, i - d)
            def _(d=d, fn=fn):
                fn(i - d - NC)
        for d, fn in ((D3, stage3), (D2, stage2), (D1, stage1)):
            @when(0, LAST, i - d)
            def _(d=d, fn=fn):
                fn(i - d)
        for k in range(NC):
            @pl.when(i == k)
            def _(k=k):
                core_arrived(a_rows, k, sem_as, sem_ar, 10 + k)

        @pl.when(i < NC)
        def _():
            dz = jnp.where(i < 2, 0, jnp.where(i >= 6, 2, jnp.where(i % 2 == 0, 3, 1)))
            other = jnp.where(i < 2, i, jnp.where(i >= 6, i - 6, (i - 2) // 2))
            q = ((z + dz) % 4) * 2 + jnp.where(other == 0, xl, xo)
            base = pl.multiple_of(q * CH, CH)
            part[i % 4] = jnp.dot(attn[pl.ds(base, CH), :], wout[...], preferred_element_type=F32)

        @when(NC, LAST, i)
        def _():
            stage0_student(i)

        @pl.when(i <= LAST)
        def _():
            stage0_send(i)
        for k in range(1, NC):
            @pl.when(i == k - 1)
            def _(k=k):
                arrive_a(k)
        for step, at in ((0, 4), (1, 6), (2, 7)):
            @pl.when(i == at)
            def _(step=step):
                arrive_s(step)

        @pl.when(i == NC - 1)
        def _():
            for k in range(NC):
                core_arrived(s_rows, k, sem_ss, sem_sr, 8 + k)

        @when(NC, LAST, i - D7)
        def _():
            stage7(i - D7 - NC)
        return carry

    lax.fori_loop(0, LAST + D7 + 1, tick, 0)

    lrecv[t] = lacc[...]
    for i in range(1, 8):
        remote(lacc, lrecv.at[t], sem_ls.at[0], sem_lr.at[0], {"tp": (t + i) % 8, "fsdp": f}).start()
    out = pltpu.make_async_copy(acc, grad_out, sem_in.at[0])
    out.start()
    for copy in sends.values():
        copy().wait_send()
    w = remote(lrecv.at[pl.ds(0, 7)], lrecv.at[pl.ds(0, 7)], sem_ls.at[0], sem_lr.at[0], CORE)
    w.wait_recv()
    w.wait_send()
    total = lrecv[0]
    for i in range(1, 8):
        total = total + lrecv[i]
    loss_ref[0, 0] = jnp.sum(total) / total_rows
    out.wait()


def local(attn_out, w_out, student, w_align, perm):
    rows_all, width = NC * CH, w_out.shape[1]
    dma = pltpu.SemaphoreType.DMA
    loss, grad = pl.pallas_call(
        kernel,
        name="distill",
        out_shape=(jax.ShapeDtypeStruct((1, 1), F32),
                   jax.ShapeDtypeStruct((w_align.shape[0], width), F32)),
        in_specs=[pl.BlockSpec(memory_space=pl.ANY)] * 4 + [pl.BlockSpec(memory_space=pltpu.VMEM)],
        out_specs=(pl.BlockSpec(memory_space=pltpu.SMEM), pl.BlockSpec(memory_space=pl.ANY)),
        scratch_shapes=[
            pltpu.VMEM((rows_all, attn_out.shape[1]), BF),
            pltpu.VMEM((rows_all, student.shape[1]), BF),
            pltpu.VMEM((rows_all, student.shape[1]), BF),
            pltpu.VMEM(w_out.shape, BF),
            pltpu.VMEM(w_align.shape, BF),
            pltpu.VMEM((4, CH, width), F32),
            pltpu.VMEM((4, 2, HF, width), BF),
            pltpu.VMEM((2 * NC, 2, HF, width), BF),
            pltpu.VMEM((4, 2, GR, width), BF),
            pltpu.VMEM((2 * NC, 2, GR, width), BF),
            pltpu.VMEM((4, HF, width), F32),
            pltpu.VMEM((2 * NC, HF, width), F32),
            pltpu.VMEM((4, HF, width), F32),
            pltpu.VMEM((NC, HF, width), BF),
            pltpu.VMEM((NC, HF, width), F32),
            pltpu.VMEM((NC, 8, 128), F32),
            pltpu.VMEM((NC, 16, 8, 128), F32),
            pltpu.VMEM((rows_all, width), BF),
            pltpu.VMEM((w_align.shape[0], width), F32),
            pltpu.VMEM((8, 128), F32),
            pltpu.VMEM((8, 8, 128), F32),
            dma((4,)),
            dma((18,)), dma((18,)), dma((16,)), dma((16,)),
            dma((4, 2)), dma((2 * NC, 2)),
            dma((4, 2)), dma((2 * NC, 2)),
            dma((8,)), dma((3 * NC,)),
            dma((NC,)), dma((NC,)),
            dma((4, 2, 2)), dma((NC, 2, 2)),
            dma((4, 2)), dma((NC, 2)),
            dma((1,)), dma((1,)),
        ],
        compiler_params=pltpu.CompilerParams(
            collective_id=0, has_side_effects=True, vmem_limit_bytes=60 * 2**20),
    )(attn_out, student, w_out, w_align, perm.reshape(1, -1))
    return loss.reshape(()), grad


def solution(mesh):
    placed = (P("fsdp", "tp"), P("tp", "fsdp"), P("fsdp", "tp"), P("tp", "fsdp"), P())
    return jax.shard_map(
        local, mesh=mesh, in_specs=placed, out_specs=(P(), P("tp", "fsdp")), check_vma=False
    )
```

```python
import functools

import jax
import jax.numpy as jnp
from jax import lax
from jax.experimental import pallas as pl
from jax.experimental.pallas import tpu as pltpu
from jax.sharding import PartitionSpec as P

MESH = pl.DeviceIdType.MESH
BF, F32 = jnp.bfloat16, jnp.float32

NC = 8
CH = 256
BL = 128
NS = 8
HB = 64
GR = 64
HF = 32
D1, D2, D3, D4, D5, D6, D7 = 2, 4, 6, 8, 10, 12, 14
LAST = 2 * NC - 1


def place():
    t, f = lax.axis_index("tp"), lax.axis_index("fsdp")
    return t // 4, t % 4, f // 4, (f // 2) % 2, f % 2, t, f


def kernel(attn_in, stu_in, wout_in, wal_in, perm_ref, loss_ref, acc_out, stu_out, g_out,
           attn, stu, stup, wout, wal, part, rsend, rrecv, nsend, nrecv, xsend, xrecv, keep,
           town, pown, stut, ssend, srecv, gall, acc, lacc, lrecv,
           sem_in, sem_as, sem_ar, sem_cs, sem_cr, sem_ss, sem_sr, sem_rs, sem_rr, sem_ns, sem_nr, sem_xs, sem_xr,
           sem_ts, sem_tr, sem_gs, sem_gr, sem_fs, sem_fr, sem_ls, sem_lr):
    xh, y, z, xl, c, t, f = place()
    total_rows = NC * CH

    def tp_dev(a, b):
        return {"tp": a * 4 + b, "fsdp": f}

    def fs_dev(a, b, d):
        return {"tp": t, "fsdp": a * 4 + b * 2 + d}

    zp, zm, z2 = (z + 1) % 4, (z + 3) % 4, (z + 2) % 4
    yp, ym = (y + 1) % 4, (y + 3) % 4
    y2 = (y + 2) % 4
    xo, ho, co = 1 - xl, 1 - xh, 1 - c
    Y_UP, Y_DN, X_HI = tp_dev(xh, yp), tp_dev(xh, ym), tp_dev(ho, y)
    Z_UP, Z_DN = fs_dev(zp, xl, c), fs_dev(zm, xl, c)
    X_LO, CORE = fs_dev(z, xo, c), fs_dev(z, xl, co)

    def remote(src, dst, ss, rs, dev):
        return pltpu.make_async_remote_copy(
            src_ref=src, dst_ref=dst, send_sem=ss, recv_sem=rs, device_id=dev, device_id_type=MESH)

    def rows(a, b, d):
        return (a * 4 + b * 2 + d) * BL

    own = rows(z, xl, c)
    loads = [
        pltpu.make_async_copy(attn_in.at[pl.ds(0, HB)], attn.at[pl.ds(c * HB, HB)], sem_in.at[0]),
        pltpu.make_async_copy(attn_in.at[pl.ds(HB, HB)], attn.at[pl.ds(BL + c * HB, HB)], sem_in.at[1]),
        pltpu.make_async_copy(wout_in, wout, sem_in.at[2]),
        pltpu.make_async_copy(stu_in, stu.at[pl.ds(own, BL)], sem_in.at[3]),
        pltpu.make_async_copy(wal_in, wal, sem_in.at[4]),
    ]
    for l in loads:
        l.start()

    barrier = pltpu.get_barrier_semaphore()
    for i in range(1, 16):
        pl.semaphore_signal(barrier, inc=1, device_id={"tp": t, "fsdp": (f + i) % 16}, device_id_type=MESH)
    for i in range(1, 8):
        pl.semaphore_signal(barrier, inc=1, device_id={"tp": (t + i) % 8, "fsdp": f}, device_id_type=MESH)
    pl.semaphore_wait(barrier, 22)

    def slot(j, d=None):
        return attn.at[pl.ds(j * BL + (c if d is None else d) * HB, HB)]

    def inp(h):
        return attn_in.at[pl.ds(h * HB, HB)]

    def s_rows(blk, d=None, off=0, n=BL):
        return stu.at[pl.ds(rows(blk[0], blk[1], c if d is None else d) + off, n)]

    sends = {}

    def go(name, copy):
        copy().start()
        sends[name] = copy

    def to_core(j):
        go(("core", j), lambda: remote(slot(j), slot(j), sem_cs.at[j], sem_cr.at[j], CORE))

    def from_core(j):
        remote(slot(j, co), slot(j, co), sem_cs.at[j], sem_cr.at[j], CORE).wait_recv()

    def hop(i, src, j, dev):
        go(("hop", i), lambda: remote(src(), slot(j), sem_as.at[i], sem_ar.at[j], dev))

    def landed(j):
        remote(slot(j), slot(j), sem_as.at[0], sem_ar.at[j], X_LO).wait_recv()

    hop(0, lambda: inp(0), 2, Z_UP)
    hop(1, lambda: inp(1), 3, Z_DN)
    hop(2, lambda: inp(0), 4, X_LO)
    hop(3, lambda: inp(1), 7, Z_UP)
    hop(4, lambda: inp(0), 6, Z_DN)
    hop(5, lambda: inp(1), 5, X_LO)
    loads[0].wait()
    loads[1].wait()
    to_core(0)
    to_core(1)

    S_OWN, S_ZM, S_ZP, S_Z2 = (z, xl), (zm, xl), (zp, xl), (z2, xl)
    S_OTHER = [(z, xo), (zm, xo), (zp, xo), (z2, xo)]

    def s_hop(i, src, j, blk, dev, off=0, n=BL):
        go(("stu", i), lambda: remote(src(), s_rows(blk, None, off, n), sem_ss.at[i], sem_sr.at[j], dev))

    def s_landed(j, blk, off=0, n=BL):
        r = s_rows(blk, None, off, n)
        remote(r, r, sem_ss.at[0], sem_sr.at[j], X_LO).wait_recv()

    def s_core(i, blk):
        go(("score", i), lambda: remote(s_rows(blk), s_rows(blk), sem_ss.at[8 + i], sem_sr.at[8 + i], CORE))

    def s_from_core(i, blk):
        r = s_rows(blk, co)
        remote(r, r, sem_ss.at[8 + i], sem_sr.at[8 + i], CORE).wait_recv()

    s_hop(0, lambda: stu_in, 0, S_OWN, Z_UP)
    s_hop(1, lambda: stu_in, 1, S_OWN, Z_DN)
    s_hop(2, lambda: stu_in, 4, S_OWN, X_LO)
    loads[2].wait()
    loads[3].wait()
    s_core(0, S_OWN)
    loads[4].wait()
    acc[...] = jnp.zeros_like(acc)
    lacc[...] = jnp.zeros_like(lacc)

    def event(e):
        if e == 1:
            landed(2)
            hop(6, lambda: slot(2), 8, Z_UP)
            to_core(2)
            landed(3)
            hop(7, lambda: slot(3), 9, Z_DN)
            to_core(3)
            landed(4)
            hop(8, lambda: slot(4), 10, Z_UP)
            to_core(4)
        elif e == 2:
            landed(5)
            hop(10, lambda: slot(5), 11, Z_DN)
            to_core(5)
            landed(6)
            to_core(6)
            landed(7)
            to_core(7)
        elif e == 3:
            s_landed(0, S_ZM)
            s_hop(3, lambda: s_rows(S_ZM, None, 0, HB), 2, S_ZM, Z_UP, 0, HB)
            s_hop(4, lambda: s_rows(S_ZM), 5, S_ZM, X_LO)
            s_core(1, S_ZM)
            s_landed(1, S_ZP)
            s_hop(5, lambda: s_rows(S_ZP, None, HB, HB), 3, S_ZP, Z_DN, HB, HB)
            s_hop(6, lambda: s_rows(S_ZP), 6, S_ZP, X_LO)
            s_core(2, S_ZP)
            hop(9, lambda: slot(4), 12, Z_DN)
            hop(11, lambda: slot(5), 13, Z_UP)
        elif e == 4:
            landed(8)
            to_core(8)
            landed(9)
            to_core(9)
        elif e == 5:
            landed(10)
            hop(12, lambda: slot(10), 14, Z_UP)
            to_core(10)
            landed(11)
            hop(13, lambda: slot(11), 15, Z_DN)
            to_core(11)
        elif e == 6:
            s_landed(2, S_Z2, 0, HB)
            s_landed(3, S_Z2, HB, HB)
            s_hop(7, lambda: s_rows(S_Z2), 7, S_Z2, X_LO)
            s_core(3, S_Z2)
        elif e == 7:
            landed(12)
            to_core(12)
            landed(13)
            to_core(13)
        elif e == 8:
            for j in range(3):
                s_landed(4 + j, S_OTHER[j])
                s_core(4 + j, S_OTHER[j])
        elif e == 9:
            landed(14)
            to_core(14)
            landed(15)
            to_core(15)
        elif e == 10:
            s_landed(7, S_OTHER[3])
            s_core(7, S_OTHER[3])
        elif e == 11:
            for i, blk in enumerate([S_OWN, S_ZM, S_ZP, S_Z2] + S_OTHER):
                s_from_core(i, blk)

    EVENTS = ((0, (1,)), (1, (2,)), (2, (3,)), (3, (4,)), (4, (5,)), (5, (6, 8, 7)), (6, (10, 9)), (7, (11,)))

    def group(ref, slot, g, off, n):
        return ref[slot, pl.ds(g * GR + off, n), :]

    def relay(r, d):
        s = r % NS
        dev = Y_UP if d == 0 else Y_DN
        return remote(rsend.at[s, d], rrecv.at[r, d], sem_rs.at[s, d], sem_rr.at[r, d], dev)

    def near(r, d):
        s = r % NS
        dev = Y_UP if d == 0 else Y_DN
        return remote(nsend.at[s, d], nrecv.at[r, d], sem_ns.at[s, d], sem_nr.at[r, d], dev)

    def across(r):
        s = r % NS
        return remote(xsend.at[s], xrecv.at[r], sem_xs.at[s], sem_xr.at[r], X_HI)

    def stage0_send(r):
        s = r % NS
        rsend[s, 0] = group(part, s, y2, 0, HF).astype(BF)
        relay(r, 0).start()
        rsend[s, 1] = group(part, s, y2, HF, HF).astype(BF)
        relay(r, 1).start()

    def stage0_student(r):
        base = pl.multiple_of((r - NC) * CH, CH)
        at = lax.broadcasted_iota(jnp.int32, (CH, 1), 0)
        row = base + ((at // GR) % 2) * BL + (at // BL) * HB + at % GR
        pick = jnp.where(row == perm_ref[...], 1.0, 0.0).astype(BF)
        mine = jnp.dot(pick, stu[...], preferred_element_type=F32).astype(BF)
        stup[pl.ds(base, CH), :] = mine
        part[r % NS] = jnp.dot(mine, wal[...], preferred_element_type=F32)

    def stage1(r):
        s = r % NS
        relay(r, 0).wait()
        nsend[s, 0, 0:HF, :] = (group(part, s, yp, 0, HF) + rrecv[r, 0].astype(F32)).astype(BF)
        nsend[s, 0, HF:GR, :] = group(part, s, yp, HF, HF).astype(BF)
        near(r, 0).start()
        relay(r, 1).wait()
        nsend[s, 1, 0:HF, :] = group(part, s, ym, 0, HF).astype(BF)
        nsend[s, 1, HF:GR, :] = (group(part, s, ym, HF, HF) + rrecv[r, 1].astype(F32)).astype(BF)
        near(r, 1).start()

    def stage2(r):
        s = r % NS
        near(r, 0).wait()
        near(r, 1).wait()

        def half(h):
            o = pl.multiple_of(h * HF, HF)
            return (group(part, s, y, o, HF) + nrecv[r, 0, pl.ds(o, HF), :].astype(F32)
                    + nrecv[r, 1, pl.ds(o, HF), :].astype(F32))

        xsend[s] = half(ho)
        across(r).start()
        keep[s] = half(xh)

    def stat_copy(k, i):
        return remote(ssend.at[k], srecv.at[k, f], sem_ts.at[k], sem_tr.at[k],
                      {"tp": t, "fsdp": (f + i) % 16})

    def lanes_of(cols):
        lane = lax.broadcasted_iota(jnp.int32, (HF, 128), 1)
        m = jnp.zeros((HF, 128), F32)
        for j, col in enumerate(cols):
            m = jnp.where(lane == j, col, m)
        m = jnp.concatenate([m, jnp.zeros((128 - HF, 128), F32)], axis=0)
        return m.T[0:8, :]

    def stage3(r):
        s = r % NS
        across(r).wait()
        full = keep[s] + xrecv[r]

        @pl.when(r < NC)
        def _():
            side = jnp.logical_or(jnp.logical_or(r == 1, r == 3), jnp.logical_or(r == 5, r == 6))
            low = jnp.logical_or(r == 1, r == 5) == (y < 2)
            dz = jnp.where(side, jnp.where(low, 3, 1), jnp.where(jnp.logical_or(r == 4, r == 7), 2, 0))
            other = jnp.logical_or(r == 2, r >= 5)
            q = ((z + dz) % 4) * 2 + jnp.where(other, xo, xl)
            town[q] = full.astype(BF)

        @pl.when(r >= NC)
        def _():
            k = r - NC
            tg = town[k].astype(F32)
            pown[k] = full
            ssend[k] = lanes_of([jnp.sum(full * tg, axis=1, keepdims=True),
                                 jnp.sum(full * full, axis=1, keepdims=True),
                                 jnp.sum(tg * tg, axis=1, keepdims=True)])
            srecv[k, f] = ssend[k]
            for i in range(1, 16):
                stat_copy(k, i).start()

    def g_rows(k, g, h):
        return gall.at[pl.ds(pl.multiple_of(k * CH + g * GR + h * HF, HF), HF)]

    def g_across(k, h):
        return remote(g_rows(k, y, h), g_rows(k, y, h), sem_xs.at[NS + k], sem_xr.at[2 * NC + k], X_HI)

    def g_near(k, d, h, g):
        return remote(g_rows(k, g, h), g_rows(k, g, h), sem_gs.at[k, d, h], sem_gr.at[k, d, h],
                      Y_UP if d == 0 else Y_DN)

    def g_far(k, d, g):
        return remote(g_rows(k, g, d), g_rows(k, g, d), sem_fs.at[k, d], sem_fr.at[k, d],
                      Y_UP if d == 0 else Y_DN)

    def stage4(k):
        w = remote(srecv.at[k, pl.ds(0, 15)], srecv.at[k, pl.ds(0, 15)], sem_ts.at[k], sem_tr.at[k], CORE)
        w.wait_recv()
        w.wait_send()
        st = srecv[k, 0]
        for i in range(1, 16):
            st = st + srecv[k, i]
        dots, pp, qq = st[0:1, :], st[1:2, :], st[2:3, :]
        n_p, n_t = jnp.sqrt(pp + 1e-6), jnp.sqrt(qq + 1e-6)
        cosine = dots / (n_p * n_t)
        lane = lax.broadcasted_iota(jnp.int32, (1, 128), 1)
        lacc[0:1, :] += jnp.where(lane < HF, 1.0 - cosine, 0.0)
        scale = 16 * 1024 / 32.0
        ca = -scale / (n_p * n_t)
        cb = scale * (cosine / (n_p * n_p))
        both = jnp.concatenate([ca, cb, jnp.zeros((126, 128), F32)], axis=0).T
        g = both[0:HF, 0:1] * town[k].astype(F32) + both[0:HF, 1:2] * pown[k]
        gall[pl.ds(pl.multiple_of(k * CH + y * GR + xh * HF, HF), HF), :] = g.astype(BF)
        g_across(k, xh).start()
        g_near(k, 0, xh, y).start()
        g_near(k, 1, xh, y).start()

        @pl.when(k == NC - 1)
        def _():
            lrecv[t] = lacc[...]
            for i in range(1, 8):
                remote(lacc, lrecv.at[t], sem_ls.at[0], sem_lr.at[0], {"tp": (t + i) % 8, "fsdp": f}).start()

    def stage5(k):
        g_across(k, xh).wait_send()
        g_across(k, ho).wait_recv()
        g_near(k, 0, ho, y).start()
        g_near(k, 1, ho, y).start()

    def stage6(k):
        g_near(k, 0, 0, ym).wait_recv()
        g_far(k, 0, ym).start()
        g_near(k, 1, 1, yp).wait_recv()
        g_far(k, 1, yp).start()

    def stage7(k):
        g_near(k, 0, 1, ym).wait_recv()
        g_near(k, 1, 0, yp).wait_recv()
        g_far(k, 0, y2).wait_recv()
        g_far(k, 1, y2).wait_recv()
        for d in range(2):
            g_far(k, d, y).wait_send()
            for h in range(2):
                g_near(k, d, h, y).wait_send()
        base = pl.multiple_of(k * CH, CH)

        @pl.when(k < NC - 1)
        def _():
            acc[...] += lax.dot_general(
                stup[pl.ds(base, CH), :], gall[pl.ds(base, CH), :], (((0,), (0,)), ((), ())),
                preferred_element_type=F32)

        @pl.when(k == NC - 2)
        def _():
            out_copy(0).start()
            stut[...] = stup[end, :].T
            out_copy(1).start()

    end = pl.ds((NC - 1) * CH, CH)

    def out_copy(i):
        src, dst = ((acc, acc_out), (stut, stu_out), (gall.at[end], g_out))[i]
        return pltpu.make_async_copy(src, dst, sem_in.at[i])

    def tick(i, carry):
        def when(lo, hi, cond_value):
            return pl.when(jnp.logical_and(cond_value >= lo, cond_value <= hi))

        for d, fn in ((D6, stage6), (D5, stage5), (D4, stage4)):
            @when(NC, LAST, i - d)
            def _(d=d, fn=fn):
                fn(i - d - NC)
        for d, fn in ((D3, stage3), (D2, stage2), (D1, stage1)):
            @when(0, LAST, i - d)
            def _(d=d, fn=fn):
                fn(i - d)
        for k in range(NC):
            @pl.when(i == k)
            def _(k=k):
                from_core(2 * k)
                from_core(2 * k + 1)

        @pl.when(i < NC)
        def _():
            base = pl.multiple_of(i * CH, CH)
            part[i % NS] = jnp.dot(attn[pl.ds(base, CH), :], wout[...], preferred_element_type=F32)

        @when(NC, LAST, i)
        def _():
            stage0_student(i)

        @pl.when(i <= LAST)
        def _():
            stage0_send(i)
        for at, events in EVENTS:
            @pl.when(i == at)
            def _(events=events):
                for e in events:
                    event(e)

        @when(NC, LAST, i - D7)
        def _():
            stage7(i - D7 - NC)
        return carry

    lax.fori_loop(0, LAST + D7 + 1, tick, 0)

    out_copy(2).start()
    for copy in sends.values():
        copy().wait_send()
    w = remote(lrecv.at[pl.ds(0, 7)], lrecv.at[pl.ds(0, 7)], sem_ls.at[0], sem_lr.at[0], CORE)
    w.wait_recv()
    w.wait_send()
    total = lrecv[0]
    for i in range(1, 8):
        total = total + lrecv[i]
    loss_ref[0, 0] = jnp.sum(total) / total_rows
    for i in range(3):
        out_copy(i).wait()


def finish(stu_ref, g_ref, acc_ref, out_ref):
    out_ref[...] = acc_ref[...] + jnp.dot(stu_ref[...], g_ref[...], preferred_element_type=F32)


def local(attn_out, w_out, student, w_align, perm):
    rows_all, width = NC * CH, w_out.shape[1]
    dma = pltpu.SemaphoreType.DMA
    loss, acc, stu_end, g_end = pl.pallas_call(
        kernel,
        name="distill",
        out_shape=(jax.ShapeDtypeStruct((1, 1), F32),
                   jax.ShapeDtypeStruct((w_align.shape[0], width), F32),
                   jax.ShapeDtypeStruct((student.shape[1], CH), BF),
                   jax.ShapeDtypeStruct((CH, width), BF)),
        in_specs=[pl.BlockSpec(memory_space=pl.ANY)] * 4 + [pl.BlockSpec(memory_space=pltpu.VMEM)],
        out_specs=(pl.BlockSpec(memory_space=pltpu.SMEM),) + (pl.BlockSpec(memory_space=pl.ANY),) * 3,
        scratch_shapes=[
            pltpu.VMEM((rows_all, attn_out.shape[1]), BF),
            pltpu.VMEM((rows_all, student.shape[1]), BF),
            pltpu.VMEM((rows_all, student.shape[1]), BF),
            pltpu.VMEM(w_out.shape, BF),
            pltpu.VMEM(w_align.shape, BF),
            pltpu.VMEM((NS, CH, width), F32),
            pltpu.VMEM((NS, 2, HF, width), BF),
            pltpu.VMEM((2 * NC, 2, HF, width), BF),
            pltpu.VMEM((NS, 2, GR, width), BF),
            pltpu.VMEM((2 * NC, 2, GR, width), BF),
            pltpu.VMEM((NS, HF, width), F32),
            pltpu.VMEM((2 * NC, HF, width), F32),
            pltpu.VMEM((NS, HF, width), F32),
            pltpu.VMEM((NC, HF, width), BF),
            pltpu.VMEM((NC, HF, width), F32),
            pltpu.VMEM((student.shape[1], CH), BF),
            pltpu.VMEM((NC, 8, 128), F32),
            pltpu.VMEM((NC, 16, 8, 128), F32),
            pltpu.VMEM((rows_all, width), BF),
            pltpu.VMEM((w_align.shape[0], width), F32),
            pltpu.VMEM((8, 128), F32),
            pltpu.VMEM((8, 8, 128), F32),
            dma((5,)),
            dma((14,)), dma((16,)), dma((16,)), dma((16,)), dma((16,)), dma((16,)),
            dma((NS, 2)), dma((2 * NC, 2)),
            dma((NS, 2)), dma((2 * NC, 2)),
            dma((NS + NC,)), dma((3 * NC,)),
            dma((NC,)), dma((NC,)),
            dma((NC, 2, 2)), dma((NC, 2, 2)),
            dma((NC, 2)), dma((NC, 2)),
            dma((1,)), dma((1,)),
        ],
        compiler_params=pltpu.CompilerParams(
            collective_id=0, has_side_effects=True, vmem_limit_bytes=60 * 2**20),
    )(attn_out, student, w_out, w_align, perm.reshape(1, -1))
    tile = 512
    grad = pl.pallas_call(
        finish,
        name="finish",
        grid=(acc.shape[0] // tile,),
        out_shape=jax.ShapeDtypeStruct(acc.shape, F32),
        in_specs=[pl.BlockSpec((tile, CH), lambda i: (i, 0)), pl.BlockSpec((CH, width), lambda i: (0, 0)),
                  pl.BlockSpec((tile, width), lambda i: (i, 0))],
        out_specs=pl.BlockSpec((tile, width), lambda i: (i, 0)),
    )(stu_end, g_end, acc)
    return loss.reshape(()), grad


def solution(mesh):
    placed = (P("fsdp", "tp"), P("tp", "fsdp"), P("fsdp", "tp"), P("tp", "fsdp"), P())
    return jax.shard_map(
        local, mesh=mesh, in_specs=placed, out_specs=(P(), P("tp", "fsdp")), check_vma=False
    )
```

```python
import functools

import jax
import jax.numpy as jnp
from jax import lax
from jax.experimental import pallas as pl
from jax.experimental.pallas import tpu as pltpu
from jax.sharding import PartitionSpec as P

MESH = pl.DeviceIdType.MESH
BF, F32 = jnp.bfloat16, jnp.float32

NC = 8
CH = 256
BL = 128
NS = 8
HB = 64
GR = 64
HF = 32
D1, D2, D3, D4, D5, D6, D7 = 2, 4, 6, 8, 10, 12, 14
LAST = 2 * NC - 1


def place():
    t, f = lax.axis_index("tp"), lax.axis_index("fsdp")
    return t // 4, t % 4, f // 4, (f // 2) % 2, f % 2, t, f


def kernel(attn_in, stu_in, wout_in, wal_in, perm_ref, loss_ref, acc_out, stu_out, g_out,
           attn, stu, stup, wout, wal, part, rsend, rrecv, nsend, nrecv, xsend, xrecv, keep,
           town, pown, stut, ssend, srecv, gall, acc, lacc, lrecv,
           sem_in, sem_as, sem_ar, sem_cs, sem_cr, sem_ss, sem_sr, sem_rs, sem_rr, sem_ns, sem_nr, sem_xs, sem_xr,
           sem_ts, sem_tr, sem_gs, sem_gr, sem_fs, sem_fr, sem_ls, sem_lr):
    xh, y, z, xl, c, t, f = place()
    total_rows = NC * CH

    def tp_dev(a, b):
        return {"tp": a * 4 + b, "fsdp": f}

    def fs_dev(a, b, d):
        return {"tp": t, "fsdp": a * 4 + b * 2 + d}

    zp, zm, z2 = (z + 1) % 4, (z + 3) % 4, (z + 2) % 4
    yp, ym = (y + 1) % 4, (y + 3) % 4
    y2 = (y + 2) % 4
    xo, ho, co = 1 - xl, 1 - xh, 1 - c
    Y_UP, Y_DN, X_HI = tp_dev(xh, yp), tp_dev(xh, ym), tp_dev(ho, y)
    Z_UP, Z_DN = fs_dev(zp, xl, c), fs_dev(zm, xl, c)
    X_LO, CORE = fs_dev(z, xo, c), fs_dev(z, xl, co)

    def remote(src, dst, ss, rs, dev):
        return pltpu.make_async_remote_copy(
            src_ref=src, dst_ref=dst, send_sem=ss, recv_sem=rs, device_id=dev, device_id_type=MESH)

    def rows(a, b, d):
        return (a * 4 + b * 2 + d) * BL

    own = rows(z, xl, c)
    loads = [
        pltpu.make_async_copy(attn_in.at[pl.ds(0, HB)], attn.at[pl.ds(c * HB, HB)], sem_in.at[0]),
        pltpu.make_async_copy(attn_in.at[pl.ds(HB, HB)], attn.at[pl.ds(BL + c * HB, HB)], sem_in.at[1]),
        pltpu.make_async_copy(wout_in, wout, sem_in.at[2]),
        pltpu.make_async_copy(stu_in, stu.at[pl.ds(own, BL)], sem_in.at[3]),
        pltpu.make_async_copy(wal_in, wal, sem_in.at[4]),
    ]
    for l in loads:
        l.start()

    barrier = pltpu.get_barrier_semaphore()
    for i in range(1, 16):
        pl.semaphore_signal(barrier, inc=1, device_id={"tp": t, "fsdp": (f + i) % 16}, device_id_type=MESH)
    for i in range(1, 8):
        pl.semaphore_signal(barrier, inc=1, device_id={"tp": (t + i) % 8, "fsdp": f}, device_id_type=MESH)
    pl.semaphore_wait(barrier, 22)

    def slot(j, d=None):
        return attn.at[pl.ds(j * BL + (c if d is None else d) * HB, HB)]

    def inp(h):
        return attn_in.at[pl.ds(h * HB, HB)]

    def s_rows(blk, d=None, off=0, n=BL):
        return stu.at[pl.ds(rows(blk[0], blk[1], c if d is None else d) + off, n)]

    sends = {}

    def go(name, copy):
        copy().start()
        sends[name] = copy

    def to_core(j):
        go(("core", j), lambda: remote(slot(j), slot(j), sem_cs.at[j], sem_cr.at[j], CORE))

    def from_core(j):
        remote(slot(j, co), slot(j, co), sem_cs.at[j], sem_cr.at[j], CORE).wait_recv()

    def hop(i, src, j, dev):
        go(("hop", i), lambda: remote(src(), slot(j), sem_as.at[i], sem_ar.at[j], dev))

    def landed(j):
        remote(slot(j), slot(j), sem_as.at[0], sem_ar.at[j], X_LO).wait_recv()

    hop(0, lambda: inp(0), 2, Z_UP)
    hop(1, lambda: inp(1), 3, Z_DN)
    hop(2, lambda: inp(0), 4, X_LO)
    hop(5, lambda: inp(1), 5, X_LO)
    loads[0].wait()
    loads[1].wait()
    to_core(0)
    to_core(1)

    S_OWN, S_ZM, S_ZP, S_Z2 = (z, xl), (zm, xl), (zp, xl), (z2, xl)
    S_OTHER = [(z, xo), (zm, xo), (zp, xo), (z2, xo)]

    def s_hop(i, src, j, blk, dev, off=0, n=BL):
        go(("stu", i), lambda: remote(src(), s_rows(blk, None, off, n), sem_ss.at[i], sem_sr.at[j], dev))

    def s_landed(j, blk, off=0, n=BL):
        r = s_rows(blk, None, off, n)
        remote(r, r, sem_ss.at[0], sem_sr.at[j], X_LO).wait_recv()

    def s_core(i, blk):
        go(("score", i), lambda: remote(s_rows(blk), s_rows(blk), sem_ss.at[8 + i], sem_sr.at[8 + i], CORE))

    def s_from_core(i, blk):
        r = s_rows(blk, co)
        remote(r, r, sem_ss.at[8 + i], sem_sr.at[8 + i], CORE).wait_recv()

    s_hop(0, lambda: stu_in, 0, S_OWN, Z_UP)
    s_hop(1, lambda: stu_in, 1, S_OWN, Z_DN)
    hop(3, lambda: inp(1), 7, Z_UP)
    hop(4, lambda: inp(0), 6, Z_DN)
    s_hop(2, lambda: stu_in, 4, S_OWN, X_LO)
    loads[2].wait()
    loads[3].wait()
    s_core(0, S_OWN)
    loads[4].wait()
    acc[...] = jnp.zeros_like(acc)
    lacc[...] = jnp.zeros_like(lacc)

    def event(e):
        if e == 1:
            landed(2)
            hop(6, lambda: slot(2), 8, Z_UP)
            to_core(2)
            landed(3)
            hop(7, lambda: slot(3), 9, Z_DN)
            to_core(3)
            landed(4)
            to_core(4)
        elif e == 2:
            hop(8, lambda: slot(4), 10, Z_UP)
            landed(5)
            hop(10, lambda: slot(5), 11, Z_DN)
            to_core(5)
            hop(9, lambda: slot(4), 12, Z_DN)
            hop(11, lambda: slot(5), 13, Z_UP)
        elif e == 12:
            landed(6)
            to_core(6)
            landed(7)
            to_core(7)
        elif e == 3:
            s_landed(0, S_ZM)
            s_hop(3, lambda: s_rows(S_ZM, None, 0, HB), 2, S_ZM, Z_UP, 0, HB)
            s_hop(4, lambda: s_rows(S_ZM), 5, S_ZM, X_LO)
            s_core(1, S_ZM)
            s_landed(1, S_ZP)
            s_hop(5, lambda: s_rows(S_ZP, None, HB, HB), 3, S_ZP, Z_DN, HB, HB)
            s_hop(6, lambda: s_rows(S_ZP), 6, S_ZP, X_LO)
            s_core(2, S_ZP)
        elif e == 4:
            landed(8)
            to_core(8)
            landed(9)
            to_core(9)
        elif e == 5:
            landed(10)
            hop(12, lambda: slot(10), 14, Z_UP)
            to_core(10)
            landed(11)
            hop(13, lambda: slot(11), 15, Z_DN)
            to_core(11)
        elif e == 6:
            s_landed(2, S_Z2, 0, HB)
            s_landed(3, S_Z2, HB, HB)
            s_hop(7, lambda: s_rows(S_Z2), 7, S_Z2, X_LO)
            s_core(3, S_Z2)
        elif e == 7:
            landed(12)
            to_core(12)
            landed(13)
            to_core(13)
        elif e == 8:
            for j in range(3):
                s_landed(4 + j, S_OTHER[j])
                s_core(4 + j, S_OTHER[j])
        elif e == 9:
            landed(14)
            to_core(14)
            landed(15)
            to_core(15)
        elif e == 10:
            s_landed(7, S_OTHER[3])
            s_core(7, S_OTHER[3])
        elif e == 11:
            for i, blk in enumerate([S_OWN, S_ZM, S_ZP, S_Z2] + S_OTHER):
                s_from_core(i, blk)

    EVENTS = ((0, (1,)), (1, (3, 2)), (2, (12,)), (3, (4,)), (4, (6, 8, 5)), (5, (10, 11)), (6, (7,)), (7, (9,)))

    def group(ref, slot, g, off, n):
        return ref[slot, pl.ds(g * GR + off, n), :]

    def relay(r, d):
        s = r % NS
        dev = Y_UP if d == 0 else Y_DN
        return remote(rsend.at[s, d], rrecv.at[r, d], sem_rs.at[s, d], sem_rr.at[r, d], dev)

    def near(r, d):
        s = r % NS
        dev = Y_UP if d == 0 else Y_DN
        return remote(nsend.at[s, d], nrecv.at[r, d], sem_ns.at[s, d], sem_nr.at[r, d], dev)

    def across(r):
        s = r % NS
        return remote(xsend.at[s], xrecv.at[r], sem_xs.at[s], sem_xr.at[r], X_HI)

    def stage0_send(r):
        s = r % NS
        rsend[s, 0] = group(part, s, y2, 0, HF).astype(BF)
        relay(r, 0).start()
        rsend[s, 1] = group(part, s, y2, HF, HF).astype(BF)
        relay(r, 1).start()

    T_AT = (0, 1, 2, 3, 4, 5, 7, 9)

    def is_teacher(r):
        return jnp.logical_or(r < 6, jnp.logical_or(r == 7, r == 9))

    def teacher_chunk(r):
        return jnp.where(r < 6, r, jnp.where(r == 7, 6, 7))

    def student_chunk(r):
        return jnp.where(r == 6, 0, jnp.where(r == 8, 1, r - NC))

    def stage0_student(r):
        base = pl.multiple_of(student_chunk(r) * CH, CH)
        at = lax.broadcasted_iota(jnp.int32, (CH, 1), 0)
        row = base + ((at // GR) % 2) * BL + (at // BL) * HB + at % GR
        pick = jnp.where(row == perm_ref[...], 1.0, 0.0).astype(BF)
        mine = jnp.dot(pick, stu[...], preferred_element_type=F32).astype(BF)
        stup[pl.ds(base, CH), :] = mine
        part[r % NS] = jnp.dot(mine, wal[...], preferred_element_type=F32)

    def stage1(r):
        s = r % NS
        relay(r, 0).wait()
        nsend[s, 0, 0:HF, :] = (group(part, s, yp, 0, HF) + rrecv[r, 0].astype(F32)).astype(BF)
        nsend[s, 0, HF:GR, :] = group(part, s, yp, HF, HF).astype(BF)
        near(r, 0).start()
        relay(r, 1).wait()
        nsend[s, 1, 0:HF, :] = group(part, s, ym, 0, HF).astype(BF)
        nsend[s, 1, HF:GR, :] = (group(part, s, ym, HF, HF) + rrecv[r, 1].astype(F32)).astype(BF)
        near(r, 1).start()

    def stage2(r):
        s = r % NS
        near(r, 0).wait()
        near(r, 1).wait()

        def half(h):
            o = pl.multiple_of(h * HF, HF)
            return (group(part, s, y, o, HF) + nrecv[r, 0, pl.ds(o, HF), :].astype(F32)
                    + nrecv[r, 1, pl.ds(o, HF), :].astype(F32))

        xsend[s] = half(ho)
        across(r).start()
        keep[s] = half(xh)

    def stat_copy(k, i):
        return remote(ssend.at[k], srecv.at[k, f], sem_ts.at[k], sem_tr.at[k],
                      {"tp": t, "fsdp": (f + i) % 16})

    def lanes_of(cols):
        lane = lax.broadcasted_iota(jnp.int32, (HF, 128), 1)
        m = jnp.zeros((HF, 128), F32)
        for j, col in enumerate(cols):
            m = jnp.where(lane == j, col, m)
        m = jnp.concatenate([m, jnp.zeros((128 - HF, 128), F32)], axis=0)
        return m.T[0:8, :]

    def stage3(r):
        s = r % NS
        across(r).wait()
        full = keep[s] + xrecv[r]

        @pl.when(is_teacher(r))
        def _():
            n = teacher_chunk(r)
            side = jnp.logical_or(jnp.logical_or(n == 1, n == 3), jnp.logical_or(n == 5, n == 6))
            low = jnp.logical_or(n == 1, n == 5) == (y < 2)
            dz = jnp.where(side, jnp.where(low, 3, 1), jnp.where(jnp.logical_or(n == 4, n == 7), 2, 0))
            other = jnp.logical_or(n == 2, n >= 5)
            q = ((z + dz) % 4) * 2 + jnp.where(other, xo, xl)
            town[q] = full.astype(BF)

        @pl.when(jnp.logical_not(is_teacher(r)))
        def _():
            pown[student_chunk(r)] = full

    def stats(k):
        tg, full = town[k].astype(F32), pown[k]
        ssend[k] = lanes_of([jnp.sum(full * tg, axis=1, keepdims=True),
                             jnp.sum(full * full, axis=1, keepdims=True),
                             jnp.sum(tg * tg, axis=1, keepdims=True)])
        srecv[k, f] = ssend[k]
        for i in range(1, 16):
            stat_copy(k, i).start()

    def g_rows(k, g, h):
        return gall.at[pl.ds(pl.multiple_of(k * CH + g * GR + h * HF, HF), HF)]

    def g_across(k, h):
        return remote(g_rows(k, y, h), g_rows(k, y, h), sem_xs.at[NS + k], sem_xr.at[2 * NC + k], X_HI)

    def g_near(k, d, h, g):
        return remote(g_rows(k, g, h), g_rows(k, g, h), sem_gs.at[k, d, h], sem_gr.at[k, d, h],
                      Y_UP if d == 0 else Y_DN)

    def g_far(k, d, g):
        return remote(g_rows(k, g, d), g_rows(k, g, d), sem_fs.at[k, d], sem_fr.at[k, d],
                      Y_UP if d == 0 else Y_DN)

    def stage4(k):
        w = remote(srecv.at[k, pl.ds(0, 15)], srecv.at[k, pl.ds(0, 15)], sem_ts.at[k], sem_tr.at[k], CORE)
        w.wait_recv()
        w.wait_send()
        st = srecv[k, 0]
        for i in range(1, 16):
            st = st + srecv[k, i]
        dots, pp, qq = st[0:1, :], st[1:2, :], st[2:3, :]
        n_p, n_t = jnp.sqrt(pp + 1e-6), jnp.sqrt(qq + 1e-6)
        cosine = dots / (n_p * n_t)
        lane = lax.broadcasted_iota(jnp.int32, (1, 128), 1)
        lacc[0:1, :] += jnp.where(lane < HF, 1.0 - cosine, 0.0)
        scale = 16 * 1024 / 32.0
        ca = -scale / (n_p * n_t)
        cb = scale * (cosine / (n_p * n_p))
        both = jnp.concatenate([ca, cb, jnp.zeros((126, 128), F32)], axis=0).T
        g = both[0:HF, 0:1] * town[k].astype(F32) + both[0:HF, 1:2] * pown[k]
        gall[pl.ds(pl.multiple_of(k * CH + y * GR + xh * HF, HF), HF), :] = g.astype(BF)
        g_across(k, xh).start()
        g_near(k, 0, xh, y).start()
        g_near(k, 1, xh, y).start()

        @pl.when(k == NC - 1)
        def _():
            lrecv[t] = lacc[...]
            for i in range(1, 8):
                remote(lacc, lrecv.at[t], sem_ls.at[0], sem_lr.at[0], {"tp": (t + i) % 8, "fsdp": f}).start()

    def stage5(k):
        g_across(k, xh).wait_send()
        g_across(k, ho).wait_recv()
        g_near(k, 0, ho, y).start()
        g_near(k, 1, ho, y).start()

    def stage6(k):
        g_near(k, 0, 0, ym).wait_recv()
        g_far(k, 0, ym).start()
        g_near(k, 1, 1, yp).wait_recv()
        g_far(k, 1, yp).start()

    def stage7(k):
        g_near(k, 0, 1, ym).wait_recv()
        g_near(k, 1, 0, yp).wait_recv()
        g_far(k, 0, y2).wait_recv()
        g_far(k, 1, y2).wait_recv()
        for d in range(2):
            g_far(k, d, y).wait_send()
            for h in range(2):
                g_near(k, d, h, y).wait_send()
        base = pl.multiple_of(k * CH, CH)

        @pl.when(k < NC - 1)
        def _():
            acc[...] += lax.dot_general(
                stup[pl.ds(base, CH), :], gall[pl.ds(base, CH), :], (((0,), (0,)), ((), ())),
                preferred_element_type=F32)

        @pl.when(k == NC - 2)
        def _():
            out_copy(0).start()
            stut[...] = stup[end, :].T
            out_copy(1).start()

    end = pl.ds((NC - 1) * CH, CH)

    def out_copy(i):
        src, dst = ((acc, acc_out), (stut, stu_out), (gall.at[end], g_out))[i]
        return pltpu.make_async_copy(src, dst, sem_in.at[i])

    def tick(i, carry):
        def when(lo, hi, cond_value):
            return pl.when(jnp.logical_and(cond_value >= lo, cond_value <= hi))

        for d, fn in ((D6, stage6), (D5, stage5), (D4, stage4)):
            @when(NC, LAST, i - d)
            def _(d=d, fn=fn):
                fn(i - d - NC)
        for d, fn in ((D3, stage3), (D2, stage2), (D1, stage1)):
            @when(0, LAST, i - d)
            def _(d=d, fn=fn):
                fn(i - d)
            if fn is stage3:
                @pl.when(i == T_AT[-1] + D3)
                def _():
                    stats(0)

                @when(1, NC - 1, i - D3 - NC)
                def _():
                    stats(i - D3 - NC)
        for k in range(NC):
            @pl.when(i == T_AT[k])
            def _(k=k):
                from_core(2 * k)
                from_core(2 * k + 1)

        @pl.when(is_teacher(i))
        def _():
            base = pl.multiple_of(teacher_chunk(i) * CH, CH)
            part[i % NS] = jnp.dot(attn[pl.ds(base, CH), :], wout[...], preferred_element_type=F32)

        @pl.when(jnp.logical_and(i <= LAST, jnp.logical_not(is_teacher(i))))
        def _():
            stage0_student(i)

        @pl.when(i <= LAST)
        def _():
            stage0_send(i)
        for at, events in EVENTS:
            @pl.when(i == at)
            def _(events=events):
                for e in events:
                    event(e)

        @when(NC, LAST, i - D7)
        def _():
            stage7(i - D7 - NC)
        return carry

    lax.fori_loop(0, LAST + D7 + 1, tick, 0)

    out_copy(2).start()
    for copy in sends.values():
        copy().wait_send()
    w = remote(lrecv.at[pl.ds(0, 7)], lrecv.at[pl.ds(0, 7)], sem_ls.at[0], sem_lr.at[0], CORE)
    w.wait_recv()
    w.wait_send()
    total = lrecv[0]
    for i in range(1, 8):
        total = total + lrecv[i]
    loss_ref[0, 0] = jnp.sum(total) / total_rows
    for i in range(3):
        out_copy(i).wait()


def finish(stu_ref, g_ref, acc_ref, out_ref):
    out_ref[...] = acc_ref[...] + jnp.dot(stu_ref[...], g_ref[...], preferred_element_type=F32)


def local(attn_out, w_out, student, w_align, perm):
    rows_all, width = NC * CH, w_out.shape[1]
    dma = pltpu.SemaphoreType.DMA
    loss, acc, stu_end, g_end = pl.pallas_call(
        kernel,
        name="distill",
        out_shape=(jax.ShapeDtypeStruct((1, 1), F32),
                   jax.ShapeDtypeStruct((w_align.shape[0], width), F32),
                   jax.ShapeDtypeStruct((student.shape[1], CH), BF),
                   jax.ShapeDtypeStruct((CH, width), BF)),
        in_specs=[pl.BlockSpec(memory_space=pl.ANY)] * 4 + [pl.BlockSpec(memory_space=pltpu.VMEM)],
        out_specs=(pl.BlockSpec(memory_space=pltpu.SMEM),) + (pl.BlockSpec(memory_space=pl.ANY),) * 3,
        scratch_shapes=[
            pltpu.VMEM((rows_all, attn_out.shape[1]), BF),
            pltpu.VMEM((rows_all, student.shape[1]), BF),
            pltpu.VMEM((rows_all, student.shape[1]), BF),
            pltpu.VMEM(w_out.shape, BF),
            pltpu.VMEM(w_align.shape, BF),
            pltpu.VMEM((NS, CH, width), F32),
            pltpu.VMEM((NS, 2, HF, width), BF),
            pltpu.VMEM((2 * NC, 2, HF, width), BF),
            pltpu.VMEM((NS, 2, GR, width), BF),
            pltpu.VMEM((2 * NC, 2, GR, width), BF),
            pltpu.VMEM((NS, HF, width), F32),
            pltpu.VMEM((2 * NC, HF, width), F32),
            pltpu.VMEM((NS, HF, width), F32),
            pltpu.VMEM((NC, HF, width), BF),
            pltpu.VMEM((NC, HF, width), F32),
            pltpu.VMEM((student.shape[1], CH), BF),
            pltpu.VMEM((NC, 8, 128), F32),
            pltpu.VMEM((NC, 16, 8, 128), F32),
            pltpu.VMEM((rows_all, width), BF),
            pltpu.VMEM((w_align.shape[0], width), F32),
            pltpu.VMEM((8, 128), F32),
            pltpu.VMEM((8, 8, 128), F32),
            dma((5,)),
            dma((14,)), dma((16,)), dma((16,)), dma((16,)), dma((16,)), dma((16,)),
            dma((NS, 2)), dma((2 * NC, 2)),
            dma((NS, 2)), dma((2 * NC, 2)),
            dma((NS + NC,)), dma((3 * NC,)),
            dma((NC,)), dma((NC,)),
            dma((NC, 2, 2)), dma((NC, 2, 2)),
            dma((NC, 2)), dma((NC, 2)),
            dma((1,)), dma((1,)),
        ],
        compiler_params=pltpu.CompilerParams(
            collective_id=0, has_side_effects=True, vmem_limit_bytes=60 * 2**20),
    )(attn_out, student, w_out, w_align, perm.reshape(1, -1))
    tile = 512
    grad = pl.pallas_call(
        finish,
        name="finish",
        grid=(acc.shape[0] // tile,),
        out_shape=jax.ShapeDtypeStruct(acc.shape, F32),
        in_specs=[pl.BlockSpec((tile, CH), lambda i: (i, 0)), pl.BlockSpec((CH, width), lambda i: (0, 0)),
                  pl.BlockSpec((tile, width), lambda i: (i, 0))],
        out_specs=pl.BlockSpec((tile, width), lambda i: (i, 0)),
    )(stu_end, g_end, acc)
    return loss.reshape(()), grad


def solution(mesh):
    placed = (P("fsdp", "tp"), P("tp", "fsdp"), P("fsdp", "tp"), P("tp", "fsdp"), P())
    return jax.shard_map(
        local, mesh=mesh, in_specs=placed, out_specs=(P(), P("tp", "fsdp")), check_vma=False
    )
```

```python
import functools

import jax
import jax.numpy as jnp
from jax import lax
from jax.experimental import pallas as pl
from jax.experimental.pallas import tpu as pltpu
from jax.sharding import PartitionSpec as P

MESH = pl.DeviceIdType.MESH
BF, F32 = jnp.bfloat16, jnp.float32

NC = 8
CH = 256
BL = 128
NS = 8
HB = 64
GR = 64
HF = 32
D1, D2, D3, D4, D5, D6, D7 = 2, 4, 6, 8, 10, 12, 14
LAST = 2 * NC - 1


def place():
    t, f = lax.axis_index("tp"), lax.axis_index("fsdp")
    return t // 4, t % 4, f // 4, (f // 2) % 2, f % 2, t, f


def kernel(attn_in, stu_in, wout_in, wal_in, perm_ref, loss_ref, acc_out, stu_out, g_out,
           attn, stu, stup, wout, wal, part, rsend, rrecv, nsend, nrecv, xsend, xrecv, keep,
           town, pown, stut, ssend, srecv, gall, acc, lacc, lrecv,
           sem_in, sem_as, sem_ar, sem_cs, sem_cr, sem_ss, sem_sr, sem_rs, sem_rr, sem_ns, sem_nr, sem_xs, sem_xr,
           sem_ts, sem_tr, sem_gs, sem_gr, sem_fs, sem_fr, sem_ls, sem_lr):
    xh, y, z, xl, c, t, f = place()
    total_rows = NC * CH

    def tp_dev(a, b):
        return {"tp": a * 4 + b, "fsdp": f}

    def fs_dev(a, b, d):
        return {"tp": t, "fsdp": a * 4 + b * 2 + d}

    zp, zm, z2 = (z + 1) % 4, (z + 3) % 4, (z + 2) % 4
    yp, ym = (y + 1) % 4, (y + 3) % 4
    y2 = (y + 2) % 4
    xo, ho, co = 1 - xl, 1 - xh, 1 - c
    Y_UP, Y_DN, X_HI = tp_dev(xh, yp), tp_dev(xh, ym), tp_dev(ho, y)
    Z_UP, Z_DN = fs_dev(zp, xl, c), fs_dev(zm, xl, c)
    X_LO, CORE = fs_dev(z, xo, c), fs_dev(z, xl, co)

    def remote(src, dst, ss, rs, dev):
        return pltpu.make_async_remote_copy(
            src_ref=src, dst_ref=dst, send_sem=ss, recv_sem=rs, device_id=dev, device_id_type=MESH)

    def rows(a, b, d):
        return (a * 4 + b * 2 + d) * BL

    own = rows(z, xl, c)
    loads = [
        pltpu.make_async_copy(attn_in.at[pl.ds(0, HB)], attn.at[pl.ds(c * HB, HB)], sem_in.at[0]),
        pltpu.make_async_copy(attn_in.at[pl.ds(HB, HB)], attn.at[pl.ds(BL + c * HB, HB)], sem_in.at[1]),
        pltpu.make_async_copy(wout_in, wout, sem_in.at[2]),
        pltpu.make_async_copy(stu_in, stu.at[pl.ds(own, BL)], sem_in.at[3]),
        pltpu.make_async_copy(wal_in, wal, sem_in.at[4]),
    ]
    for l in loads:
        l.start()

    barrier = pltpu.get_barrier_semaphore()
    for i in range(1, 16):
        pl.semaphore_signal(barrier, inc=1, device_id={"tp": t, "fsdp": (f + i) % 16}, device_id_type=MESH)
    for i in range(1, 8):
        pl.semaphore_signal(barrier, inc=1, device_id={"tp": (t + i) % 8, "fsdp": f}, device_id_type=MESH)
    pl.semaphore_wait(barrier, 22)

    def slot(j, d=None):
        return attn.at[pl.ds(j * BL + (c if d is None else d) * HB, HB)]

    def inp(h):
        return attn_in.at[pl.ds(h * HB, HB)]

    def s_rows(blk, d=None, off=0, n=BL):
        return stu.at[pl.ds(rows(blk[0], blk[1], c if d is None else d) + off, n)]

    sends = {}

    def go(name, copy):
        copy().start()
        sends[name] = copy

    def to_core(j):
        go(("core", j), lambda: remote(slot(j), slot(j), sem_cs.at[j], sem_cr.at[j], CORE))

    def from_core(j):
        remote(slot(j, co), slot(j, co), sem_cs.at[j], sem_cr.at[j], CORE).wait_recv()

    def hop(i, src, j, dev):
        go(("hop", i), lambda: remote(src(), slot(j), sem_as.at[i], sem_ar.at[j], dev))

    def landed(j):
        remote(slot(j), slot(j), sem_as.at[0], sem_ar.at[j], X_LO).wait_recv()

    hop(0, lambda: inp(0), 2, Z_UP)
    hop(1, lambda: inp(1), 3, Z_DN)
    hop(2, lambda: inp(0), 4, X_LO)
    hop(5, lambda: inp(1), 5, X_LO)
    loads[0].wait()
    loads[1].wait()
    to_core(0)
    to_core(1)

    S_OWN, S_ZM, S_ZP, S_Z2 = (z, xl), (zm, xl), (zp, xl), (z2, xl)
    S_OTHER = [(z, xo), (zm, xo), (zp, xo), (z2, xo)]

    def s_hop(i, src, j, blk, dev, off=0, n=BL):
        go(("stu", i), lambda: remote(src(), s_rows(blk, None, off, n), sem_ss.at[i], sem_sr.at[j], dev))

    def s_landed(j, blk, off=0, n=BL):
        r = s_rows(blk, None, off, n)
        remote(r, r, sem_ss.at[0], sem_sr.at[j], X_LO).wait_recv()

    def s_core(i, blk):
        go(("score", i), lambda: remote(s_rows(blk), s_rows(blk), sem_ss.at[8 + i], sem_sr.at[8 + i], CORE))

    def s_from_core(i, blk):
        r = s_rows(blk, co)
        remote(r, r, sem_ss.at[8 + i], sem_sr.at[8 + i], CORE).wait_recv()

    s_hop(0, lambda: stu_in, 0, S_OWN, Z_UP)
    s_hop(1, lambda: stu_in, 1, S_OWN, Z_DN)
    hop(3, lambda: inp(1), 7, Z_UP)
    hop(4, lambda: inp(0), 6, Z_DN)
    s_hop(2, lambda: stu_in, 4, S_OWN, X_LO)
    loads[2].wait()
    loads[3].wait()
    s_core(0, S_OWN)
    lacc[...] = jnp.zeros_like(lacc)

    def event(e):
        if e == 1:
            landed(2)
            hop(6, lambda: slot(2), 8, Z_UP)
            to_core(2)
            landed(3)
            hop(7, lambda: slot(3), 9, Z_DN)
            to_core(3)
            landed(4)
            to_core(4)
        elif e == 2:
            hop(8, lambda: slot(4), 10, Z_UP)
            landed(5)
            hop(10, lambda: slot(5), 11, Z_DN)
            to_core(5)
            hop(9, lambda: slot(4), 12, Z_DN)
            hop(11, lambda: slot(5), 13, Z_UP)
        elif e == 12:
            landed(6)
            to_core(6)
            landed(7)
            to_core(7)
        elif e == 3:
            s_landed(0, S_ZM)
            s_hop(3, lambda: s_rows(S_ZM, None, 0, HB), 2, S_ZM, Z_UP, 0, HB)
            s_hop(4, lambda: s_rows(S_ZM), 5, S_ZM, X_LO)
            s_core(1, S_ZM)
            s_landed(1, S_ZP)
            s_hop(5, lambda: s_rows(S_ZP, None, HB, HB), 3, S_ZP, Z_DN, HB, HB)
            s_hop(6, lambda: s_rows(S_ZP), 6, S_ZP, X_LO)
            s_core(2, S_ZP)
        elif e == 4:
            landed(8)
            to_core(8)
            landed(9)
            to_core(9)
        elif e == 5:
            landed(10)
            hop(12, lambda: slot(10), 14, Z_UP)
            to_core(10)
            landed(11)
            hop(13, lambda: slot(11), 15, Z_DN)
            to_core(11)
        elif e == 6:
            s_landed(2, S_Z2, 0, HB)
            s_landed(3, S_Z2, HB, HB)
            s_hop(7, lambda: s_rows(S_Z2), 7, S_Z2, X_LO)
            s_core(3, S_Z2)
        elif e == 7:
            landed(12)
            to_core(12)
            landed(13)
            to_core(13)
        elif e == 8:
            for j in range(3):
                s_landed(4 + j, S_OTHER[j])
                s_core(4 + j, S_OTHER[j])
        elif e == 9:
            landed(14)
            to_core(14)
            landed(15)
            to_core(15)
        elif e == 10:
            s_landed(7, S_OTHER[3])
            s_core(7, S_OTHER[3])
        elif e == 11:
            loads[4].wait()
            for i, blk in enumerate([S_OWN, S_ZM, S_ZP, S_Z2] + S_OTHER):
                s_from_core(i, blk)

    EVENTS = ((0, (1,)), (1, (3, 2)), (2, (12,)), (3, (4,)), (4, (6, 8, 5)), (5, (10, 11)), (6, (7,)), (7, (9,)))

    def group(ref, slot, g, off, n):
        return ref[slot, pl.ds(g * GR + off, n), :]

    def relay(r, d):
        s = r % NS
        dev = Y_UP if d == 0 else Y_DN
        return remote(rsend.at[s, d], rrecv.at[r, d], sem_rs.at[s, d], sem_rr.at[r, d], dev)

    def near(r, d):
        s = r % NS
        dev = Y_UP if d == 0 else Y_DN
        return remote(nsend.at[s, d], nrecv.at[r, d], sem_ns.at[s, d], sem_nr.at[r, d], dev)

    def across(r):
        s = r % NS
        return remote(xsend.at[s], xrecv.at[r], sem_xs.at[s], sem_xr.at[r], X_HI)

    def stage0_send(r):
        s = r % NS
        rsend[s, 0] = group(part, s, y2, 0, HF).astype(BF)
        relay(r, 0).start()
        rsend[s, 1] = group(part, s, y2, HF, HF).astype(BF)
        relay(r, 1).start()

    T_AT = (0, 1, 2, 3, 4, 5, 7, 9)

    def is_teacher(r):
        return jnp.logical_or(r < 6, jnp.logical_or(r == 7, r == 9))

    def teacher_chunk(r):
        return jnp.where(r < 6, r, jnp.where(r == 7, 6, 7))

    def student_chunk(r):
        return jnp.where(r == 6, 0, jnp.where(r == 8, 1, r - NC))

    def stage0_student(r):
        base = pl.multiple_of(student_chunk(r) * CH, CH)
        at = lax.broadcasted_iota(jnp.int32, (CH, 1), 0)
        row = base + ((at // GR) % 2) * BL + (at // BL) * HB + at % GR
        pick = jnp.where(row == perm_ref[...], 1.0, 0.0).astype(BF)
        mine = jnp.dot(pick, stu[...], preferred_element_type=F32).astype(BF)
        stup[pl.ds(base, CH), :] = mine
        part[r % NS] = jnp.dot(mine, wal[...], preferred_element_type=F32)

    def stage1(r):
        s = r % NS
        relay(r, 0).wait()
        nsend[s, 0, 0:HF, :] = (group(part, s, yp, 0, HF) + rrecv[r, 0].astype(F32)).astype(BF)
        nsend[s, 0, HF:GR, :] = group(part, s, yp, HF, HF).astype(BF)
        near(r, 0).start()
        relay(r, 1).wait()
        nsend[s, 1, 0:HF, :] = group(part, s, ym, 0, HF).astype(BF)
        nsend[s, 1, HF:GR, :] = (group(part, s, ym, HF, HF) + rrecv[r, 1].astype(F32)).astype(BF)
        near(r, 1).start()

    def stage2(r):
        s = r % NS
        near(r, 0).wait()
        near(r, 1).wait()

        def half(h):
            o = pl.multiple_of(h * HF, HF)
            return (group(part, s, y, o, HF) + nrecv[r, 0, pl.ds(o, HF), :].astype(F32)
                    + nrecv[r, 1, pl.ds(o, HF), :].astype(F32))

        xsend[s] = half(ho)
        across(r).start()
        keep[s] = half(xh)

    def stat_copy(k, i):
        return remote(ssend.at[k], srecv.at[k, f], sem_ts.at[k], sem_tr.at[k],
                      {"tp": t, "fsdp": (f + i) % 16})

    def lanes_of(cols):
        lane = lax.broadcasted_iota(jnp.int32, (HF, 128), 1)
        m = jnp.zeros((HF, 128), F32)
        for j, col in enumerate(cols):
            m = jnp.where(lane == j, col, m)
        m = jnp.concatenate([m, jnp.zeros((128 - HF, 128), F32)], axis=0)
        return m.T[0:8, :]

    def stage3(r):
        s = r % NS
        across(r).wait()
        full = keep[s] + xrecv[r]

        @pl.when(is_teacher(r))
        def _():
            n = teacher_chunk(r)
            side = jnp.logical_or(jnp.logical_or(n == 1, n == 3), jnp.logical_or(n == 5, n == 6))
            low = jnp.logical_or(n == 1, n == 5) == (y < 2)
            dz = jnp.where(side, jnp.where(low, 3, 1), jnp.where(jnp.logical_or(n == 4, n == 7), 2, 0))
            other = jnp.logical_or(n == 2, n >= 5)
            q = ((z + dz) % 4) * 2 + jnp.where(other, xo, xl)
            town[q] = full.astype(BF)

        @pl.when(jnp.logical_not(is_teacher(r)))
        def _():
            pown[student_chunk(r)] = full

    def stats(k):
        tg, full = town[k].astype(F32), pown[k]
        ssend[k] = lanes_of([jnp.sum(full * tg, axis=1, keepdims=True),
                             jnp.sum(full * full, axis=1, keepdims=True),
                             jnp.sum(tg * tg, axis=1, keepdims=True)])
        srecv[k, f] = ssend[k]
        for i in range(1, 16):
            stat_copy(k, i).start()

    def g_rows(k, g, h):
        return gall.at[pl.ds(pl.multiple_of(k * CH + g * GR + h * HF, HF), HF)]

    def g_across(k, h):
        return remote(g_rows(k, y, h), g_rows(k, y, h), sem_xs.at[NS + k], sem_xr.at[2 * NC + k], X_HI)

    def g_near(k, d, h, g):
        return remote(g_rows(k, g, h), g_rows(k, g, h), sem_gs.at[k, d, h], sem_gr.at[k, d, h],
                      Y_UP if d == 0 else Y_DN)

    def g_far(k, d, g):
        return remote(g_rows(k, g, d), g_rows(k, g, d), sem_fs.at[k, d], sem_fr.at[k, d],
                      Y_UP if d == 0 else Y_DN)

    def stage4(k):
        w = remote(srecv.at[k, pl.ds(0, 15)], srecv.at[k, pl.ds(0, 15)], sem_ts.at[k], sem_tr.at[k], CORE)
        w.wait_recv()
        w.wait_send()
        st = srecv[k, 0]
        for i in range(1, 16):
            st = st + srecv[k, i]
        dots, pp, qq = st[0:1, :], st[1:2, :], st[2:3, :]
        n_p, n_t = jnp.sqrt(pp + 1e-6), jnp.sqrt(qq + 1e-6)
        cosine = dots / (n_p * n_t)
        lane = lax.broadcasted_iota(jnp.int32, (1, 128), 1)
        lacc[0:1, :] += jnp.where(lane < HF, 1.0 - cosine, 0.0)
        scale = 16 * 1024 / 32.0
        ca = -scale / (n_p * n_t)
        cb = scale * (cosine / (n_p * n_p))
        both = jnp.concatenate([ca, cb, jnp.zeros((126, 128), F32)], axis=0).T
        g = both[0:HF, 0:1] * town[k].astype(F32) + both[0:HF, 1:2] * pown[k]
        gall[pl.ds(pl.multiple_of(k * CH + y * GR + xh * HF, HF), HF), :] = g.astype(BF)
        g_across(k, xh).start()
        g_near(k, 0, xh, y).start()
        g_near(k, 1, xh, y).start()

        @pl.when(k == NC - 1)
        def _():
            lrecv[t] = lacc[...]
            for i in range(1, 8):
                remote(lacc, lrecv.at[t], sem_ls.at[0], sem_lr.at[0], {"tp": (t + i) % 8, "fsdp": f}).start()

    def stage5(k):
        g_across(k, xh).wait_send()
        g_across(k, ho).wait_recv()
        g_near(k, 0, ho, y).start()
        g_near(k, 1, ho, y).start()

    def stage6(k):
        g_near(k, 0, 0, ym).wait_recv()
        g_far(k, 0, ym).start()
        g_near(k, 1, 1, yp).wait_recv()
        g_far(k, 1, yp).start()

    def stage7(k):
        g_near(k, 0, 1, ym).wait_recv()
        g_near(k, 1, 0, yp).wait_recv()
        g_far(k, 0, y2).wait_recv()
        g_far(k, 1, y2).wait_recv()
        for d in range(2):
            g_far(k, d, y).wait_send()
            for h in range(2):
                g_near(k, d, h, y).wait_send()
        base = pl.multiple_of(k * CH, CH)

        def product():
            return lax.dot_general(
                stup[pl.ds(base, CH), :], gall[pl.ds(base, CH), :], (((0,), (0,)), ((), ())),
                preferred_element_type=F32)

        @pl.when(k == 0)
        def _():
            acc[...] = product()

        @pl.when(jnp.logical_and(k > 0, k < NC - 1))
        def _():
            acc[...] += product()

        @pl.when(k == NC - 2)
        def _():
            out_copy(0).start()
            stut[...] = stup[end, :].T
            out_copy(1).start()

    end = pl.ds((NC - 1) * CH, CH)

    def out_copy(i):
        src, dst = ((acc, acc_out), (stut, stu_out), (gall.at[end], g_out))[i]
        return pltpu.make_async_copy(src, dst, sem_in.at[i])

    def tick(i, carry):
        def when(lo, hi, cond_value):
            return pl.when(jnp.logical_and(cond_value >= lo, cond_value <= hi))

        for d, fn in ((D6, stage6), (D5, stage5), (D4, stage4)):
            @when(NC, LAST, i - d)
            def _(d=d, fn=fn):
                fn(i - d - NC)
        for d, fn in ((D3, stage3), (D2, stage2), (D1, stage1)):
            @when(0, LAST, i - d)
            def _(d=d, fn=fn):
                fn(i - d)
            if fn is stage3:
                @pl.when(i == T_AT[-1] + D3)
                def _():
                    stats(0)

                @when(1, NC - 1, i - D3 - NC)
                def _():
                    stats(i - D3 - NC)
        for k in range(NC):
            @pl.when(i == T_AT[k])
            def _(k=k):
                from_core(2 * k)
                from_core(2 * k + 1)

        @pl.when(is_teacher(i))
        def _():
            base = pl.multiple_of(teacher_chunk(i) * CH, CH)
            part[i % NS] = jnp.dot(attn[pl.ds(base, CH), :], wout[...], preferred_element_type=F32)

        @pl.when(jnp.logical_and(i <= LAST, jnp.logical_not(is_teacher(i))))
        def _():
            stage0_student(i)

        @pl.when(i <= LAST)
        def _():
            stage0_send(i)
        for at, events in EVENTS:
            @pl.when(i == at)
            def _(events=events):
                for e in events:
                    event(e)

        @when(NC, LAST, i - D7)
        def _():
            stage7(i - D7 - NC)
        return carry

    lax.fori_loop(0, LAST + D7 + 1, tick, 0)

    out_copy(2).start()
    for copy in sends.values():
        copy().wait_send()
    w = remote(lrecv.at[pl.ds(0, 7)], lrecv.at[pl.ds(0, 7)], sem_ls.at[0], sem_lr.at[0], CORE)
    w.wait_recv()
    w.wait_send()
    total = lrecv[0]
    for i in range(1, 8):
        total = total + lrecv[i]
    loss_ref[0, 0] = jnp.sum(total) / total_rows
    for i in range(3):
        out_copy(i).wait()


def finish(stu_ref, g_ref, acc_ref, out_ref):
    out_ref[...] = acc_ref[...] + jnp.dot(stu_ref[...], g_ref[...], preferred_element_type=F32)


def local(attn_out, w_out, student, w_align, perm):
    rows_all, width = NC * CH, w_out.shape[1]
    dma = pltpu.SemaphoreType.DMA
    loss, acc, stu_end, g_end = pl.pallas_call(
        kernel,
        name="distill",
        out_shape=(jax.ShapeDtypeStruct((1, 1), F32),
                   jax.ShapeDtypeStruct((w_align.shape[0], width), F32),
                   jax.ShapeDtypeStruct((student.shape[1], CH), BF),
                   jax.ShapeDtypeStruct((CH, width), BF)),
        in_specs=[pl.BlockSpec(memory_space=pl.ANY)] * 4 + [pl.BlockSpec(memory_space=pltpu.VMEM)],
        out_specs=(pl.BlockSpec(memory_space=pltpu.SMEM),) + (pl.BlockSpec(memory_space=pl.ANY),) * 3,
        scratch_shapes=[
            pltpu.VMEM((rows_all, attn_out.shape[1]), BF),
            pltpu.VMEM((rows_all, student.shape[1]), BF),
            pltpu.VMEM((rows_all, student.shape[1]), BF),
            pltpu.VMEM(w_out.shape, BF),
            pltpu.VMEM(w_align.shape, BF),
            pltpu.VMEM((NS, CH, width), F32),
            pltpu.VMEM((NS, 2, HF, width), BF),
            pltpu.VMEM((2 * NC, 2, HF, width), BF),
            pltpu.VMEM((NS, 2, GR, width), BF),
            pltpu.VMEM((2 * NC, 2, GR, width), BF),
            pltpu.VMEM((NS, HF, width), F32),
            pltpu.VMEM((2 * NC, HF, width), F32),
            pltpu.VMEM((NS, HF, width), F32),
            pltpu.VMEM((NC, HF, width), BF),
            pltpu.VMEM((NC, HF, width), F32),
            pltpu.VMEM((student.shape[1], CH), BF),
            pltpu.VMEM((NC, 8, 128), F32),
            pltpu.VMEM((NC, 16, 8, 128), F32),
            pltpu.VMEM((rows_all, width), BF),
            pltpu.VMEM((w_align.shape[0], width), F32),
            pltpu.VMEM((8, 128), F32),
            pltpu.VMEM((8, 8, 128), F32),
            dma((5,)),
            dma((14,)), dma((16,)), dma((16,)), dma((16,)), dma((16,)), dma((16,)),
            dma((NS, 2)), dma((2 * NC, 2)),
            dma((NS, 2)), dma((2 * NC, 2)),
            dma((NS + NC,)), dma((3 * NC,)),
            dma((NC,)), dma((NC,)),
            dma((NC, 2, 2)), dma((NC, 2, 2)),
            dma((NC, 2)), dma((NC, 2)),
            dma((1,)), dma((1,)),
        ],
        compiler_params=pltpu.CompilerParams(
            collective_id=0, has_side_effects=True, vmem_limit_bytes=60 * 2**20),
    )(attn_out, student, w_out, w_align, perm.reshape(1, -1))
    tile = 512
    grad = pl.pallas_call(
        finish,
        name="finish",
        grid=(acc.shape[0] // tile,),
        out_shape=jax.ShapeDtypeStruct(acc.shape, F32),
        in_specs=[pl.BlockSpec((tile, CH), lambda i: (i, 0)), pl.BlockSpec((CH, width), lambda i: (0, 0)),
                  pl.BlockSpec((tile, width), lambda i: (i, 0))],
        out_specs=pl.BlockSpec((tile, width), lambda i: (i, 0)),
    )(stu_end, g_end, acc)
    return loss.reshape(()), grad


def solution(mesh):
    placed = (P("fsdp", "tp"), P("tp", "fsdp"), P("fsdp", "tp"), P("tp", "fsdp"), P())
    return jax.shard_map(
        local, mesh=mesh, in_specs=placed, out_specs=(P(), P("tp", "fsdp")), check_vma=False
    )
```
